32 devices in a mesh: groups: 2 (over y), loop: 4 (over z), rep: 4 (over x, core).
Axes of the slice: x: 2, y: 2, z: 4, core: 2. Of those that a mesh axis runs over, the one named last changes fastest.
Arguments:
- features: bfloat16 [8192, 512], P(('groups', 'loop', 'rep')), parts along dimension 0, may hold values from -6 to 6
- weight: bfloat16 [512, 512], replicated, may hold values from -0.25 to 0.25
- block_row: int32 [8, 4, 4, 6], P(('groups', 'loop'), 'rep'), parts along dimension 0, may hold values from 0 to 7
- edge_row: int32 [8, 4, 4, 6, 64], P(('groups', 'loop'), 'rep'), parts along dimension 0, may hold values from 0 to 127
- edge_col: int32 [8, 4, 4, 6, 64], P(('groups', 'loop'), 'rep'), parts along dimension 0, may hold values from 0 to 255
- edge_count: int32 [8, 4, 4, 6, 64], P(('groups', 'loop'), 'rep'), parts along dimension 0, may hold values from 1 to 3
Outputs:
- activated: bfloat16 [8192, 512], P(('groups', 'loop', 'rep')), parts along dimension 0
The draws below stay inside these ranges and needn't reach their ends.
There are 2 independent parts, one for each index of `groups`. The reference program is written for one: setup_inputs(seed, part) draws one part's arguments, and reference() takes and returns one part's arrays. A program takes and returns all parts, laid end to end along the dimension named above; an argument that names none is the same for every part. Nothing has to cross between parts.
All inputs are finite; a program needn't handle non-finite values.
Results may differ from the reference program's by a relative error of at most 0.0085.
Values may be sent and summed in bfloat16 or wider, within the bound.
A program may use at most 64 MiB of HBM per device.

```python
import math
import jax
import jax.numpy as jnp
import numpy as np
from jax import lax

F = 512
BLOCK = 128
SLOTS = 6
EDGES = 64
ROWS_DEV = 256
ROW_BLOCKS = 8
NODES = 4096
N_LOOP = 4
N_REP = 4


def place_ends(result, stream_key, smallest, largest):
    place = [jax.random.randint(jax.random.fold_in(stream_key, axis), (), 0, length) for axis, length in enumerate(result.shape)]
    main_axis = result.shape.index(max(result.shape))
    neighbour = place[:main_axis] + [(place[main_axis] + 1) % result.shape[main_axis]] + place[main_axis + 1:]
    return result.at[tuple(place)].set(smallest).at[tuple(neighbour)].set(largest)


def block_scale(rng, dims, split, low, top_value):
    def one(position, parts):
        steps = jax.random.uniform(jax.random.fold_in(jax.random.fold_in(rng, 6), position), (parts,), jnp.float32, low / len(split), top_value / len(split))
        return jnp.repeat(jnp.exp(steps), dims[position] // parts).reshape((-1,) + (1,) * (len(dims) - position - 1))

    loudness = one(*split[0])
    for cut in split[1:]:
        loudness = loudness * one(*cut)
    return loudness


def rank_table(count, skew):
    weights = [(1 << 20) // math.isqrt(standing ** skew) + 1 for standing in range(1, count + 1)]
    scale = 1 + sum(weights) // (1 << 30)
    return np.cumsum(np.array([max(1, weight // scale) for weight in weights]))


def ranked_ids(key, dims, number_of, slope):
    grid = rank_table(number_of, slope)
    lot = jax.random.randint(jax.random.fold_in(key, 1), dims, 0, int(grid[number_of - 1]))
    standing = jnp.searchsorted(jnp.asarray(grid, jnp.int32), lot, side="right")
    return jax.random.permutation(jax.random.fold_in(key, 2), number_of)[standing].astype(jnp.int32)


def normal_values(own_key, shape, spread, limit, cuts=(), held_as=jnp.bfloat16):
    entries = spread * jax.random.normal(own_key, shape, jnp.float32)
    if cuts:
        entries = entries * block_scale(own_key, shape, cuts, -0.22, 0.18)
    return jnp.clip(entries, -limit, limit).astype(held_as)


def setup_inputs(seed: int = 0, part: int = 0) -> dict:
    key_list = jax.random.split(jax.random.key(seed), 7)
    own_keys = jax.random.split(jax.random.fold_in(key_list[6], part), 7)
    features = normal_values(own_keys[0], (NODES, F), 1.0, 6.0, ((0, 16),))
    weight = normal_values(key_list[1], (F, F), F ** -0.5, 0.25)
    block_row = place_ends(ranked_ids(own_keys[2], (N_LOOP, N_REP, N_LOOP, SLOTS), ROW_BLOCKS, 2), jax.random.fold_in(own_keys[2], 3), 0, ROW_BLOCKS - 1).astype(jnp.int32)
    edge_row = place_ends(jax.random.randint(own_keys[3], (N_LOOP, N_REP, N_LOOP, SLOTS, EDGES), 0, BLOCK), jax.random.fold_in(own_keys[3], 1), 0, BLOCK - 1).astype(jnp.int32)
    edge_col = place_ends(jax.random.randint(own_keys[4], (N_LOOP, N_REP, N_LOOP, SLOTS, EDGES), 0, ROWS_DEV), jax.random.fold_in(own_keys[4], 1), 0, ROWS_DEV - 1).astype(jnp.int32)
    edge_count = place_ends(jax.random.randint(own_keys[5], (N_LOOP, N_REP, N_LOOP, SLOTS, EDGES), 1, 4), jax.random.fold_in(own_keys[5], 1), 1, 3).astype(jnp.int32)
    return {"features": features, "weight": weight, "block_row": block_row, "edge_row": edge_row, "edge_col": edge_col, "edge_count": edge_count}


def reference(features, weight, block_row, edge_row, edge_col, edge_count):
    loop_ids = jnp.arange(N_LOOP, dtype=jnp.int32)[:, None, None, None]
    source_ids = jnp.arange(N_LOOP, dtype=jnp.int32)[None, :, None, None]
    rows_by_share = jnp.moveaxis(block_row, 1, 0)
    erow_by_share = jnp.moveaxis(edge_row, 1, 0)
    ecol_by_share = jnp.moveaxis(edge_col, 1, 0)
    count_by_share = jnp.moveaxis(edge_count, 1, 0)
    share_ids = jnp.arange(N_REP, dtype=jnp.int32)
    width = features.shape[1]

    def one_share(carry, packed):
        agg_total, deg_total = carry
        share, brow, erow, ecol, ecount = packed
        targets = loop_ids * (ROW_BLOCKS * BLOCK) + brow[..., None] * BLOCK + erow
        sources = (source_ids * N_REP + share) * ROWS_DEV + ecol
        targets = targets.reshape(-1).astype(jnp.int32)
        sources = sources.reshape(-1).astype(jnp.int32)
        counts = ecount.reshape(-1).astype(jnp.float32)
        degree_part = jax.ops.segment_sum(counts, targets, num_segments=NODES).astype(jnp.bfloat16)
        gathered = features[sources].astype(jnp.float32) * counts[:, None]
        agg_part = jax.ops.segment_sum(gathered, targets, num_segments=NODES).astype(jnp.bfloat16)
        return (agg_total + agg_part.astype(jnp.float32), deg_total + degree_part.astype(jnp.float32)), None

    start = (jnp.zeros((NODES, width), jnp.float32), jnp.zeros((NODES,), jnp.float32))
    (aggregate, degree), unused = lax.scan(one_share, start, (share_ids, rows_by_share, erow_by_share, ecol_by_share, count_by_share))
    normalized = ((aggregate + features.astype(jnp.float32)) / (degree[:, None] + 1.0)).astype(jnp.bfloat16)
    product = jnp.dot(normalized, weight, preferred_element_type=jnp.float32)
    return jnp.maximum(product, 0.0).astype(jnp.bfloat16)
```

```python
import functools

import jax
import jax.numpy as jnp
from jax import lax
from jax.experimental import pallas as pl
from jax.experimental.pallas import tpu as pltpu
from jax.sharding import PartitionSpec as P

BLOCK = 128
CHUNK = 128
MESH = pl.DeviceIdType.MESH
NT = (((1,), (1,)), ((), ()))


def repeat(count, step, most=4):
    if count <= most:
        for index in range(count):
            step(index)
    else:
        lax.fori_loop(0, count, lambda index, carry: (step(index), carry)[1], 0)


def kernel(
    loops, reps,
    feat_hbm, weight_hbm, brow_hbm, erow_hbm, ecol_hbm, ecnt_hbm,
    out_ref,
    gathered, adjacency, part_out, part_in, deg_out, deg_in, normal,
    weight_v, brow_s, erow_v, ecol_v, ecnt_v,
    local_sem, up_send, down_send, gather_recv, part_send, part_recv, deg_send, deg_recv,
):
    own, width = feat_hbm.shape
    chunks = width // CHUNK
    slots, edges = erow_v.shape[1:]
    z = lax.axis_index("loop")
    me = lax.axis_index("rep")
    has_up = z < loops - 1
    has_down = z > 0

    def rows(index):
        return pl.ds(pl.multiple_of(index * own, own), own)

    small = [
        pltpu.make_async_copy(brow_hbm, brow_s, local_sem.at[0]),
        pltpu.make_async_copy(erow_hbm, erow_v, local_sem.at[1]),
        pltpu.make_async_copy(ecol_hbm, ecol_v, local_sem.at[2]),
        pltpu.make_async_copy(ecnt_hbm, ecnt_v, local_sem.at[3]),
    ]
    weight_copy = pltpu.make_async_copy(weight_hbm, weight_v, local_sem.at[4])
    own_copy = [
        pltpu.make_async_copy(
            feat_hbm.at[:, pl.ds(c * CHUNK, CHUNK)], gathered.at[c, rows(z)], local_sem.at[5 + c]
        )
        for c in range(chunks)
    ]
    for copy in own_copy + small + [weight_copy]:
        copy.start()

    barrier = pltpu.get_barrier_semaphore()

    @pl.when(has_up)
    def _():
        pl.semaphore_signal(barrier, inc=1, device_id={"loop": z + 1}, device_id_type=MESH)

    @pl.when(has_down)
    def _():
        pl.semaphore_signal(barrier, inc=1, device_id={"loop": z - 1}, device_id_type=MESH)

    for k in range(1, reps):
        pl.semaphore_signal(
            barrier, inc=1, device_id={"rep": lax.rem(me + k, reps)}, device_id_type=MESH
        )
    pl.semaphore_wait(barrier, reps - 1 + has_up.astype(jnp.int32) + has_down.astype(jnp.int32))

    def shift(source, c, up):
        return pltpu.make_async_remote_copy(
            src_ref=gathered.at[c, rows(source)],
            dst_ref=gathered.at[c, rows(source)],
            send_sem=(up_send if up else down_send).at[source, c],
            recv_sem=gather_recv.at[source, c],
            device_id={"loop": z + 1 if up else z - 1},
            device_id_type=MESH,
        )

    for c in range(chunks):
        own_copy[c].wait()

        @pl.when(has_up)
        def _():
            shift(z, c, True).start()

        @pl.when(has_down)
        def _():
            shift(z, c, False).start()

    for copy in small:
        copy.wait()
    listed = slots * edges
    target_pos = lax.broadcasted_iota(jnp.int32, (own, listed), 0)
    source_pos = lax.broadcasted_iota(jnp.int32, (own, listed), 0)
    ones = jnp.ones((8, listed), jnp.bfloat16)

    def joined(ref, source, offset=None):
        pieces = []
        for s in range(slots):
            piece = ref[source, s : s + 1, :]
            if offset is not None:
                piece = piece + offset(s)
            pieces.append(piece)
        return jnp.concatenate(pieces, axis=1)

    deg_out[...] = jnp.zeros_like(deg_out)

    def build(source):
        target = joined(erow_v, source, lambda s: brow_s[source, s] * BLOCK)
        column = joined(ecol_v, source)
        count = joined(ecnt_v, source).astype(jnp.float32)
        pick = jnp.where(source_pos == column, 1.0, 0.0).astype(jnp.bfloat16)

        def build_rows(r):
            place = jnp.where(target_pos == target - r * own, count, 0.0).astype(jnp.bfloat16)
            block = lax.dot_general(place, pick, NT, preferred_element_type=jnp.float32)
            adjacency[rows(r), rows(source)] = block.astype(jnp.bfloat16)
            deg_out[r] += lax.dot_general(ones, place, NT, preferred_element_type=jnp.float32)

        repeat(reps, build_rows)

    repeat(loops, build)

    def deg_copy(r):
        return pltpu.make_async_remote_copy(
            src_ref=deg_out.at[r],
            dst_ref=deg_in.at[me],
            send_sem=deg_send.at[r],
            recv_sem=deg_recv.at[me],
            device_id={"rep": r},
            device_id_type=MESH,
        )

    def deg_arrival(r):
        return pltpu.make_async_remote_copy(
            src_ref=deg_out.at[r],
            dst_ref=deg_in.at[r],
            send_sem=deg_send.at[r],
            recv_sem=deg_recv.at[r],
            device_id={"rep": r},
            device_id_type=MESH,
        )

    deg_out[...] = deg_out[...].astype(jnp.bfloat16).astype(jnp.float32)
    deg_in[me] = deg_out[me]
    for k in range(1, reps):
        deg_copy(lax.rem(me + k, reps)).start()

    def gather(c):
        def hop(index):
            below = z - 1 - index
            above = z + 1 + index

            @pl.when(below >= 0)
            def _():
                copy = shift(below, c, True)
                copy.wait_recv()

                @pl.when(has_up)
                def _():
                    copy.start()

            @pl.when(above < loops)
            def _():
                copy = shift(above, c, False)
                copy.wait_recv()

                @pl.when(has_down)
                def _():
                    copy.start()

        repeat(loops - 1, hop)

    seg = min(loops, 4) * own
    segs = loops * own // seg

    def product(c, r):
        def part(index):
            span = pl.ds(pl.multiple_of(index * seg, seg), seg)
            return jnp.dot(
                adjacency[rows(r), span], gathered[c, span, :], preferred_element_type=jnp.float32
            )

        if segs == 1:
            return part(0)
        return lax.fori_loop(
            0, segs, lambda index, total: total + part(index), jnp.zeros((own, CHUNK), jnp.float32)
        )

    def part_copy(c, r, slot):
        return pltpu.make_async_remote_copy(
            src_ref=part_out.at[c, r],
            dst_ref=part_in.at[c, slot],
            send_sem=part_send.at[c, r],
            recv_sem=part_recv.at[c, slot],
            device_id={"rep": r},
            device_id_type=MESH,
        )

    def spread(c):
        def send(index):
            r = lax.rem(me + reps - 1 - index, reps)
            part_out[c, r] = product(c, r).astype(jnp.bfloat16)
            part_copy(c, r, me).start()

        repeat(reps - 1, send)
        part_in[c, me] = product(c, me).astype(jnp.bfloat16)

    scale = []

    def finish(c):
        if not scale:
            for k in range(1, reps):
                deg_arrival(lax.rem(me + k, reps)).wait_recv()
            degree = deg_in[0]
            for r in range(1, reps):
                degree += deg_in[r]
            degree = jnp.broadcast_to(degree[0:1, :] + 1.0, (CHUNK, own))
            scale.append(degree.T)
        for k in range(1, reps):
            r = lax.rem(me + k, reps)
            part_copy(c, r, r).wait_recv()
        total = gathered[c, rows(z), :].astype(jnp.float32)
        for r in range(reps):
            total += part_in[c, r].astype(jnp.float32)
        normal[:, c * CHUNK : (c + 1) * CHUNK] = (total / scale[0]).astype(jnp.bfloat16)

    for c in range(chunks):
        gather(c)
        spread(c)
        if c > 0:
            finish(c - 1)
    finish(chunks - 1)

    weight_copy.wait()
    result = jnp.dot(normal[...], weight_v[...], preferred_element_type=jnp.float32)
    out_ref[...] = jnp.maximum(result, 0.0).astype(out_ref.dtype)

    for k in range(1, reps):
        deg_copy(lax.rem(me + k, reps)).wait_send()
    for c in range(chunks):
        for k in range(1, reps):
            part_copy(c, lax.rem(me + k, reps), me).wait_send()

        def drain(source):
            @pl.when(jnp.logical_and(has_up, source <= z))
            def _():
                shift(source, c, True).wait_send()

            @pl.when(jnp.logical_and(has_down, source >= z))
            def _():
                shift(source, c, False).wait_send()

        repeat(loops, drain)


def body(features, weight, block_row, edge_row, edge_col, edge_count):
    loops = lax.axis_size("loop")
    reps = lax.axis_size("rep")
    own, width = features.shape
    chunks = width // CHUNK
    slots, edges = edge_row.shape[3:]
    listing = (loops, slots, edges)
    dma = pltpu.SemaphoreType.DMA
    return pl.pallas_call(
        functools.partial(kernel, loops, reps),
        out_shape=jax.ShapeDtypeStruct((own, weight.shape[1]), jnp.bfloat16),
        in_specs=[pl.BlockSpec(memory_space=pl.ANY)] * 6,
        out_specs=pl.BlockSpec(memory_space=pltpu.VMEM),
        scratch_shapes=[
            pltpu.VMEM((chunks, loops * own, CHUNK), jnp.bfloat16),
            pltpu.VMEM((reps * own, loops * own), jnp.bfloat16),
            pltpu.VMEM((chunks, reps, own, CHUNK), jnp.bfloat16),
            pltpu.VMEM((chunks, reps, own, CHUNK), jnp.bfloat16),
            pltpu.VMEM((reps, 8, own), jnp.float32),
            pltpu.VMEM((reps, 8, own), jnp.float32),
            pltpu.VMEM((own, width), jnp.bfloat16),
            pltpu.VMEM(weight.shape, jnp.bfloat16),
            pltpu.SMEM((loops, slots), jnp.int32),
            pltpu.VMEM(listing, jnp.int32),
            pltpu.VMEM(listing, jnp.int32),
            pltpu.VMEM(listing, jnp.int32),
            dma((5 + chunks,)),
            dma((loops, chunks)),
            dma((loops, chunks)),
            dma((loops, chunks)),
            dma((chunks, reps)),
            dma((chunks, reps)),
            dma((reps,)),
            dma((reps,)),
        ],
        compiler_params=pltpu.CompilerParams(
            collective_id=0, has_side_effects=True, vmem_limit_bytes=56 * 1024 * 1024
        ),
    )(
        features,
        weight,
        block_row.reshape(loops, slots),
        edge_row.reshape(listing),
        edge_col.reshape(listing),
        edge_count.reshape(listing),
    )


def solution(mesh):
    return jax.shard_map(
        body,
        mesh=mesh,
        in_specs=(
            P(("groups", "loop", "rep"), None),
            P(),
            P(("groups", "loop"), "rep", None, None),
            P(("groups", "loop"), "rep", None, None, None),
            P(("groups", "loop"), "rep", None, None, None),
            P(("groups", "loop"), "rep", None, None, None),
        ),
        out_specs=P(("groups", "loop", "rep"), None),
        check_vma=False,
    )
```

```python
import functools

import jax
import jax.numpy as jnp
from jax import lax
from jax.experimental import pallas as pl
from jax.experimental.pallas import tpu as pltpu
from jax.sharding import PartitionSpec as P

BLOCK = 128
CHUNK = 128
MESH = pl.DeviceIdType.MESH
NT = (((1,), (1,)), ((), ()))


def repeat(count, step, most=4):
    if count <= most:
        for index in range(count):
            step(index)
    else:
        lax.fori_loop(0, count, lambda index, carry: (step(index), carry)[1], 0)


def when(condition, step):
    if condition is True:
        step()
    elif condition is not False:
        pl.when(condition)(step)


def kernel(
    loops, reps, helped,
    feat_hbm, brow_hbm, erow_hbm, ecol_hbm, ecnt_hbm,
    out_ref,
    gathered, adjacency, mine, sib_out, sib_in, chip_out, chip_in, kept, end_out, end_in,
    deg_out, deg_in, scale, brow_v, lists, end_lists,
    local_sem, up_send, down_send, gather_recv, sib_send, sib_recv, chip_send, chip_recv,
    end_send, end_recv, list_send, list_recv, deg_send, deg_recv,
):
    own, width = feat_hbm.shape
    chunks = width // CHUNK
    slots, _, edges = erow_hbm.shape
    cores = 2 if reps % 2 == 0 else 1
    chips = reps // cores
    z = lax.axis_index("loop")
    me = lax.axis_index("rep")
    chip = lax.div(me, cores)
    core = lax.rem(me, cores)
    has_up = z < loops - 1
    has_down = z > 0
    inner = jnp.logical_and(has_up, has_down)
    at_end = jnp.logical_not(inner)
    helps_low = z == 1
    helps = jnp.logical_or(helps_low, z == loops - 2)
    end_z = jnp.where(helps_low, 0, loops - 1)
    helper_z = jnp.where(has_down, loops - 2, 1)

    def rows(index):
        return pl.ds(pl.multiple_of(index * own, own), own)

    small = [
        pltpu.make_async_copy(brow_hbm, brow_v, local_sem.at[0]),
        pltpu.make_async_copy(erow_hbm, lists.at[0], local_sem.at[1]),
        pltpu.make_async_copy(ecol_hbm, lists.at[1], local_sem.at[2]),
        pltpu.make_async_copy(ecnt_hbm, lists.at[2], local_sem.at[3]),
    ]
    own_copy = [
        pltpu.make_async_copy(
            feat_hbm.at[:, pl.ds(c * CHUNK, CHUNK)], gathered.at[c, rows(z)], local_sem.at[4 + c]
        )
        for c in range(chunks)
    ]
    for copy in own_copy + small:
        copy.start()

    barrier = pltpu.get_barrier_semaphore()

    @pl.when(has_up)
    def _():
        pl.semaphore_signal(barrier, inc=1, device_id={"loop": z + 1}, device_id_type=MESH)

    @pl.when(has_down)
    def _():
        pl.semaphore_signal(barrier, inc=1, device_id={"loop": z - 1}, device_id_type=MESH)

    for k in range(1, reps):
        pl.semaphore_signal(
            barrier, inc=1, device_id={"rep": lax.rem(me + k, reps)}, device_id_type=MESH
        )

    for copy in small:
        copy.wait()
    for s in range(slots):
        lists[0, s] = lists[0, s] + brow_v[:, s : s + 1] * BLOCK
    for c in range(chunks):
        own_copy[c].wait()
    pl.semaphore_wait(barrier, reps - 1 + has_up.astype(jnp.int32) + has_down.astype(jnp.int32))

    def shift(source, c, up):
        return pltpu.make_async_remote_copy(
            src_ref=gathered.at[c, rows(source)],
            dst_ref=gathered.at[c, rows(source)],
            send_sem=(up_send if up else down_send).at[source, c],
            recv_sem=gather_recv.at[source, c],
            device_id={"loop": z + 1 if up else z - 1},
            device_id_type=MESH,
        )

    def sends(c, up):
        if c < helped:
            return z + 1 < loops - 1 if up else z - 1 > 0
        return has_up if up else has_down

    def takes(c):
        return inner if c < helped else True

    def send_own(c, up, condition):
        when(jnp.logical_and(sends(c, up), condition), lambda: shift(z, c, up).start())

    ahead = 2

    def early(up):
        if not helped:
            return z == (0 if up else loops - 1)
        return jnp.logical_or(at_end, z + 1 == loops - 1 if up else z - 1 == 0)

    for c in range(chunks):
        for up in (True, False):
            send_own(c, up, c < ahead or early(up))

    def list_copy(kind, to):
        return pltpu.make_async_remote_copy(
            src_ref=lists.at[kind],
            dst_ref=end_lists.at[kind],
            send_sem=list_send.at[kind],
            recv_sem=list_recv.at[kind],
            device_id={"loop": to},
            device_id_type=MESH,
        )

    if helped:

        @pl.when(at_end)
        def _():
            for kind in range(3):
                list_copy(kind, helper_z).start()

    listed = slots * edges
    position = lax.broadcasted_iota(jnp.int32, (own, listed), 0)
    ones = jnp.ones((8, listed), jnp.bfloat16)
    deg_out[...] = jnp.zeros_like(deg_out)

    def build(held, which, source):
        def joined(kind):
            return jnp.concatenate(
                [held[kind, s, pl.ds(source, 1), :] for s in range(slots)], axis=1
            )

        target = joined(0)
        column = joined(1)
        count = joined(2).astype(jnp.float32)
        pick = jnp.where(position == column, 1.0, 0.0).astype(jnp.bfloat16)

        def build_rows(r):
            place = jnp.where(position == target - r * own, count, 0.0).astype(jnp.bfloat16)
            block = lax.dot_general(place, pick, NT, preferred_element_type=jnp.float32)
            adjacency[which, rows(r), rows(source)] = block.astype(jnp.bfloat16)
            if which == 0:
                deg_out[r] += lax.dot_general(ones, place, NT, preferred_element_type=jnp.float32)

        repeat(reps, build_rows)

    repeat(loops, lambda source: build(lists, 0, source))

    def deg_copy(r, slot):
        return pltpu.make_async_remote_copy(
            src_ref=deg_out.at[r],
            dst_ref=deg_in.at[slot],
            send_sem=deg_send.at[r],
            recv_sem=deg_recv.at[slot],
            device_id={"rep": r},
            device_id_type=MESH,
        )

    deg_out[...] = deg_out[...].astype(jnp.bfloat16).astype(jnp.float32)
    deg_in[me] = deg_out[me]
    for k in range(1, reps):
        deg_copy(lax.rem(me + k, reps), me).start()

    if helped:

        @pl.when(helps)
        def _():
            for kind in range(3):
                list_copy(kind, end_z).wait_recv()
            repeat(loops, lambda source: build(end_lists, 1, source))

    def gather(c):
        def hop(index):
            below = z - 1 - index
            above = z + 1 + index

            @pl.when(below >= 0)
            def _():
                shift(below, c, True).wait_recv()
                when(sends(c, True), lambda: shift(below, c, True).start())

            @pl.when(above < loops)
            def _():
                shift(above, c, False).wait_recv()
                when(sends(c, False), lambda: shift(above, c, False).start())

        repeat(loops - 1, hop)

    seg = min(loops, 4) * own
    segs = loops * own // seg

    def product(which, c, r):
        def part(index):
            span = pl.ds(pl.multiple_of(index * seg, seg), seg)
            return jnp.dot(
                adjacency[which, rows(r), span],
                gathered[c, span, :],
                preferred_element_type=jnp.float32,
            )

        if segs == 1:
            return part(0)
        return lax.fori_loop(
            0, segs, lambda index, total: total + part(index), jnp.zeros((own, CHUNK), jnp.float32)
        )

    def sib_copy(job):
        return pltpu.make_async_remote_copy(
            src_ref=sib_out.at[job],
            dst_ref=sib_in.at[job],
            send_sem=sib_send.at[job],
            recv_sem=sib_recv.at[job],
            device_id={"rep": chip * cores + 1 - core},
            device_id_type=MESH,
        )

    def chip_copy(job, other, slot):
        return pltpu.make_async_remote_copy(
            src_ref=chip_out.at[job, other],
            dst_ref=chip_in.at[job, slot],
            send_sem=chip_send.at[job, other],
            recv_sem=chip_recv.at[job, slot],
            device_id={"rep": other * cores + core},
            device_id_type=MESH,
        )

    def end_copy(c, to):
        return pltpu.make_async_remote_copy(
            src_ref=end_out.at[c],
            dst_ref=end_in.at[c],
            send_sem=end_send.at[c],
            recv_sem=end_recv.at[c],
            device_id={"loop": to},
            device_id_type=MESH,
        )

    def multiply(which, c):
        job = which * chunks + c

        if cores == 2:

            def theirs(x):
                value = product(which, c, x * cores + 1 - core)
                sib_out[job, x] = value.astype(jnp.bfloat16)

            repeat(chips, theirs)
            sib_copy(job).start()

        def ours(x):
            mine[which, x] = product(which, c, x * cores + core)

        repeat(chips, ours)

    def cross(which, c):
        job = which * chunks + c
        if cores == 2:
            sib_copy(job).wait_recv()

        def summed(x):
            total = mine[which, x]
            if cores == 2:
                total += sib_in[job, x].astype(jnp.float32)
            return total

        def send(index):
            other = lax.rem(chip + 1 + index, chips)
            chip_out[job, other] = summed(other).astype(jnp.bfloat16)
            chip_copy(job, other, chip).start()

        repeat(chips - 1, send)
        kept[job] = summed(chip)

    def received(which, c):
        job = which * chunks + c
        total = kept[job]
        for k in range(1, chips):
            other = lax.rem(chip + k, chips)
            chip_copy(job, other, other).wait_recv()
            total += chip_in[job, other].astype(jnp.float32)
        return total

    def put(c, total):
        total += gathered[c, rows(z), :].astype(jnp.float32)
        out_ref[:, c * CHUNK : (c + 1) * CHUNK] = (total / scale[...]).astype(jnp.bfloat16)

    def start_job(c):
        if c < helped:
            pl.when(helps)(lambda: multiply(1, c))
        multiply(0, c)
        if c < helped:
            pl.when(helps)(lambda: cross(1, c))
        cross(0, c)

    def end_job(c):
        if c < helped:

            @pl.when(helps)
            def _():
                end_out[c] = received(1, c).astype(jnp.bfloat16)
                end_copy(c, end_z).start()

        put(c, received(0, c))

    def degrees():
        for k in range(1, reps):
            r = lax.rem(me + k, reps)
            deg_copy(r, r).wait_recv()
        degree = deg_in[0]
        for r in range(1, reps):
            degree += deg_in[r]
        scale[...] = jnp.broadcast_to(degree[0:1, :] + 1.0, (CHUNK, own)).T

    for c in range(chunks):

        def step(c=c):
            gather(c)
            if c + ahead < chunks:
                for up in (True, False):
                    send_own(c + ahead, up, jnp.logical_not(early(up)))
            start_job(c)

        when(takes(c), step)
        if c == 0:
            degrees()
        if c > 0:
            when(takes(c - 1), lambda: end_job(c - 1))
    if helped:

        @pl.when(at_end)
        def _():
            for c in range(helped):
                end_copy(c, helper_z).wait_recv()
                put(c, end_in[c].astype(jnp.float32))

    end_job(chunks - 1)

    for k in range(1, reps):
        deg_copy(lax.rem(me + k, reps), me).wait_send()
    if helped:

        @pl.when(at_end)
        def _():
            for kind in range(3):
                list_copy(kind, helper_z).wait_send()

    def job_left(job):
        if cores == 2:
            sib_copy(job).wait_send()
        for k in range(1, chips):
            chip_copy(job, lax.rem(chip + k, chips), chip).wait_send()

    for c in range(chunks):
        when(takes(c), lambda: job_left(c))
        if c < helped:

            @pl.when(helps)
            def _():
                job_left(chunks + c)
                end_copy(c, end_z).wait_send()

        def drain(source):
            when(
                jnp.logical_and(sends(c, True), source <= z),
                lambda: shift(source, c, True).wait_send(),
            )
            when(
                jnp.logical_and(sends(c, False), source >= z),
                lambda: shift(source, c, False).wait_send(),
            )

        repeat(loops, drain)


def body(features, weight, block_row, edge_row, edge_col, edge_count):
    loops = lax.axis_size("loop")
    reps = lax.axis_size("rep")
    own, width = features.shape
    chunks = width // CHUNK
    slots, edges = edge_row.shape[3:]
    chips = reps // 2 if reps % 2 == 0 else reps
    adjacency_bytes = reps * own * loops * own * 2
    helped = chunks // 2 if loops >= 4 and adjacency_bytes <= 8 * 1024 * 1024 else 0
    kinds = 2 if helped else 1
    jobs = chunks + helped
    listing = (slots, loops, edges)
    dma = pltpu.SemaphoreType.DMA
    bf16, f32, i32 = jnp.bfloat16, jnp.float32, jnp.int32

    def stored(array):
        return jnp.swapaxes(array.reshape(loops, slots, edges), 0, 1)

    normalized = pl.pallas_call(
        functools.partial(kernel, loops, reps, helped),
        out_shape=jax.ShapeDtypeStruct((own, width), bf16),
        in_specs=[pl.BlockSpec(memory_space=pl.ANY)] * 5,
        out_specs=pl.BlockSpec(memory_space=pltpu.VMEM),
        scratch_shapes=[
            pltpu.VMEM((chunks, loops * own, CHUNK), bf16),
            pltpu.VMEM((kinds, reps * own, loops * own), bf16),
            pltpu.VMEM((kinds, chips, own, CHUNK), f32),
            pltpu.VMEM((jobs, chips, own, CHUNK), bf16),
            pltpu.VMEM((jobs, chips, own, CHUNK), bf16),
            pltpu.VMEM((jobs, chips, own, CHUNK), bf16),
            pltpu.VMEM((jobs, chips, own, CHUNK), bf16),
            pltpu.VMEM((jobs, own, CHUNK), f32),
            pltpu.VMEM((max(helped, 1), own, CHUNK), bf16),
            pltpu.VMEM((max(helped, 1), own, CHUNK), bf16),
            pltpu.VMEM((reps, 8, own), f32),
            pltpu.VMEM((reps, 8, own), f32),
            pltpu.VMEM((own, CHUNK), f32),
            pltpu.VMEM((loops, slots), i32),
            pltpu.VMEM((3,) + listing, i32),
            pltpu.VMEM((3,) + listing, i32),
            dma((4 + chunks,)),
            dma((loops, chunks)),
            dma((loops, chunks)),
            dma((loops, chunks)),
            dma((jobs,)),
            dma((jobs,)),
            dma((jobs, chips)),
            dma((jobs, chips)),
            dma((max(helped, 1),)),
            dma((max(helped, 1),)),
            dma((3,)),
            dma((3,)),
            dma((reps,)),
            dma((reps,)),
        ],
        compiler_params=pltpu.CompilerParams(
            collective_id=0, has_side_effects=True, vmem_limit_bytes=56 * 1024 * 1024
        ),
    )(
        features,
        block_row.reshape(loops, slots),
        stored(edge_row),
        stored(edge_col),
        stored(edge_count),
    )
    product = jnp.dot(normalized, weight, preferred_element_type=f32)
    return jnp.maximum(product, 0.0).astype(bf16)


def solution(mesh):
    return jax.shard_map(
        body,
        mesh=mesh,
        in_specs=(
            P(("groups", "loop", "rep"), None),
            P(),
            P(("groups", "loop"), "rep", None, None),
            P(("groups", "loop"), "rep", None, None, None),
            P(("groups", "loop"), "rep", None, None, None),
            P(("groups", "loop"), "rep", None, None, None),
        ),
        out_specs=P(("groups", "loop", "rep"), None),
        check_vma=False,
    )
```

```python
import functools

import jax
import jax.numpy as jnp
from jax import lax
from jax.experimental import pallas as pl
from jax.experimental.pallas import tpu as pltpu
from jax.sharding import PartitionSpec as P

BLOCK = 128
CHUNK = 256
MESH = pl.DeviceIdType.MESH
NT = (((1,), (1,)), ((), ()))


def repeat(count, step, most=4):
    if count <= most:
        for index in range(count):
            step(index)
    else:
        lax.fori_loop(0, count, lambda index, carry: (step(index), carry)[1], 0)


def when(condition, step):
    if condition is True:
        step()
    elif condition is not False:
        pl.when(condition)(step)


def kernel(
    loops, reps, helped,
    feat_hbm, brow_hbm, erow_hbm, ecol_hbm, ecnt_hbm,
    out_ref,
    gathered, adjacency, mine, sib_out, sib_in, chip_out, chip_in, kept, end_out, end_in,
    deg_out, deg_in, scale, brow_v, lists, end_lists,
    local_sem, up_send, down_send, gather_recv, sib_send, sib_recv, chip_send, chip_recv,
    end_send, end_recv, list_send, list_recv, deg_send, deg_recv,
):
    own, width = feat_hbm.shape
    chunks = width // CHUNK
    slots, _, edges = erow_hbm.shape
    cores = 2 if reps % 2 == 0 else 1
    chips = reps // cores
    z = lax.axis_index("loop")
    me = lax.axis_index("rep")
    chip = lax.div(me, cores)
    core = lax.rem(me, cores)
    has_up = z < loops - 1
    has_down = z > 0
    inner = jnp.logical_and(has_up, has_down)
    at_end = jnp.logical_not(inner)
    helps_low = z == 1
    helps = jnp.logical_or(helps_low, z == loops - 2)
    end_z = jnp.where(helps_low, 0, loops - 1)
    helper_z = jnp.where(has_down, loops - 2, 1)

    def rows(index):
        return pl.ds(pl.multiple_of(index * own, own), own)

    small = [
        pltpu.make_async_copy(brow_hbm, brow_v, local_sem.at[0]),
        pltpu.make_async_copy(erow_hbm, lists.at[0], local_sem.at[1]),
        pltpu.make_async_copy(ecol_hbm, lists.at[1], local_sem.at[2]),
        pltpu.make_async_copy(ecnt_hbm, lists.at[2], local_sem.at[3]),
    ]
    own_copy = [
        pltpu.make_async_copy(
            feat_hbm.at[:, pl.ds(c * CHUNK, CHUNK)], gathered.at[c, rows(z)], local_sem.at[4 + c]
        )
        for c in range(chunks)
    ]
    for copy in own_copy + small:
        copy.start()

    barrier = pltpu.get_barrier_semaphore()

    @pl.when(has_up)
    def _():
        pl.semaphore_signal(barrier, inc=1, device_id={"loop": z + 1}, device_id_type=MESH)

    @pl.when(has_down)
    def _():
        pl.semaphore_signal(barrier, inc=1, device_id={"loop": z - 1}, device_id_type=MESH)

    for k in range(1, reps):
        pl.semaphore_signal(
            barrier, inc=1, device_id={"rep": lax.rem(me + k, reps)}, device_id_type=MESH
        )

    for copy in small:
        copy.wait()
    for s in range(slots):
        lists[0, s] = lists[0, s] + brow_v[:, s : s + 1] * BLOCK
    for c in range(chunks):
        own_copy[c].wait()
    pl.semaphore_wait(barrier, reps - 1 + has_up.astype(jnp.int32) + has_down.astype(jnp.int32))

    def shift(source, c, up):
        return pltpu.make_async_remote_copy(
            src_ref=gathered.at[c, rows(source)],
            dst_ref=gathered.at[c, rows(source)],
            send_sem=(up_send if up else down_send).at[source, c],
            recv_sem=gather_recv.at[source, c],
            device_id={"loop": z + 1 if up else z - 1},
            device_id_type=MESH,
        )

    def sends(c, up):
        if c < helped:
            return z + 1 < loops - 1 if up else z - 1 > 0
        return has_up if up else has_down

    def takes(c):
        return inner if c < helped else True

    def list_copy(kind, to):
        return pltpu.make_async_remote_copy(
            src_ref=lists.at[kind],
            dst_ref=end_lists.at[kind],
            send_sem=list_send.at[kind],
            recv_sem=list_recv.at[kind],
            device_id={"loop": to},
            device_id_type=MESH,
        )

    if helped:

        @pl.when(at_end)
        def _():
            for kind in range(3):
                list_copy(kind, helper_z).start()

    for c in range(chunks):
        for up in (True, False):
            when(sends(c, up), lambda: shift(z, c, up).start())

    listed = slots * edges
    position = lax.broadcasted_iota(jnp.int32, (own, listed), 0)
    ones = jnp.ones((8, listed), jnp.bfloat16)
    deg_out[...] = jnp.zeros_like(deg_out)

    def build(held, which, source):
        def joined(kind):
            return jnp.concatenate(
                [held[kind, s, pl.ds(source, 1), :] for s in range(slots)], axis=1
            )

        target = joined(0)
        column = joined(1)
        count = joined(2).astype(jnp.float32)
        pick = jnp.where(position == column, 1.0, 0.0).astype(jnp.bfloat16)

        def build_rows(r):
            place = jnp.where(position == target - r * own, count, 0.0).astype(jnp.bfloat16)
            block = lax.dot_general(place, pick, NT, preferred_element_type=jnp.float32)
            adjacency[which, rows(r), rows(source)] = block.astype(jnp.bfloat16)
            if which == 0:
                deg_out[r] += lax.dot_general(ones, place, NT, preferred_element_type=jnp.float32)

        repeat(reps, build_rows)

    repeat(loops, lambda source: build(lists, 0, source))

    def deg_copy(r, slot):
        return pltpu.make_async_remote_copy(
            src_ref=deg_out.at[r],
            dst_ref=deg_in.at[slot],
            send_sem=deg_send.at[r],
            recv_sem=deg_recv.at[slot],
            device_id={"rep": r},
            device_id_type=MESH,
        )

    deg_out[...] = deg_out[...].astype(jnp.bfloat16).astype(jnp.float32)
    deg_in[me] = deg_out[me]
    for k in range(1, reps):
        deg_copy(lax.rem(me + k, reps), me).start()

    if helped:

        @pl.when(helps)
        def _():
            for kind in range(3):
                list_copy(kind, end_z).wait_recv()
            repeat(loops, lambda source: build(end_lists, 1, source))

    def hop(c, index):
        below = z - 1 - index
        above = z + 1 + index

        @pl.when(below >= 0)
        def _():
            shift(below, c, True).wait_recv()
            when(sends(c, True), lambda: shift(below, c, True).start())

        @pl.when(above < loops)
        def _():
            shift(above, c, False).wait_recv()
            when(sends(c, False), lambda: shift(above, c, False).start())

    for c in range(chunks):
        when(takes(c), lambda: hop(c, 0))

    def gather(c):
        repeat(loops - 2, lambda index: hop(c, index + 1))

    seg = min(loops, 4) * own
    segs = loops * own // seg

    def product(which, c, r):
        def part(index):
            span = pl.ds(pl.multiple_of(index * seg, seg), seg)
            return jnp.dot(
                adjacency[which, rows(r), span],
                gathered[c, span, :],
                preferred_element_type=jnp.float32,
            )

        if segs == 1:
            return part(0)
        return lax.fori_loop(
            0, segs, lambda index, total: total + part(index), jnp.zeros((own, CHUNK), jnp.float32)
        )

    def sib_copy(job):
        return pltpu.make_async_remote_copy(
            src_ref=sib_out.at[job],
            dst_ref=sib_in.at[job],
            send_sem=sib_send.at[job],
            recv_sem=sib_recv.at[job],
            device_id={"rep": chip * cores + 1 - core},
            device_id_type=MESH,
        )

    def chip_copy(job, other, slot):
        return pltpu.make_async_remote_copy(
            src_ref=chip_out.at[job, other],
            dst_ref=chip_in.at[job, slot],
            send_sem=chip_send.at[job, other],
            recv_sem=chip_recv.at[job, slot],
            device_id={"rep": other * cores + core},
            device_id_type=MESH,
        )

    def end_copy(c, to):
        return pltpu.make_async_remote_copy(
            src_ref=end_out.at[c],
            dst_ref=end_in.at[c],
            send_sem=end_send.at[c],
            recv_sem=end_recv.at[c],
            device_id={"loop": to},
            device_id_type=MESH,
        )

    def multiply(which, c):
        job = which * chunks + c

        if cores == 2:

            def theirs(x):
                value = product(which, c, x * cores + 1 - core)
                sib_out[job, x] = value.astype(jnp.bfloat16)

            repeat(chips, theirs)
            sib_copy(job).start()

        def ours(x):
            mine[which, x] = product(which, c, x * cores + core)

        repeat(chips, ours)

    def cross(which, c):
        job = which * chunks + c
        if cores == 2:
            sib_copy(job).wait_recv()

        def summed(x):
            total = mine[which, x]
            if cores == 2:
                total += sib_in[job, x].astype(jnp.float32)
            return total

        def send(index):
            other = lax.rem(chip + 1 + index, chips)
            chip_out[job, other] = summed(other).astype(jnp.bfloat16)
            chip_copy(job, other, chip).start()

        repeat(chips - 1, send)
        kept[job] = summed(chip)

    def received(which, c):
        job = which * chunks + c
        total = kept[job]
        for k in range(1, chips):
            other = lax.rem(chip + k, chips)
            chip_copy(job, other, other).wait_recv()
            total += chip_in[job, other].astype(jnp.float32)
        return total

    def put(c, total):
        total += gathered[c, rows(z), :].astype(jnp.float32)
        out_ref[:, c * CHUNK : (c + 1) * CHUNK] = (total / scale[...]).astype(jnp.bfloat16)

    def start_job(c):
        if c < helped:
            pl.when(helps)(lambda: multiply(1, c))
        multiply(0, c)
        if c < helped:
            pl.when(helps)(lambda: cross(1, c))
        cross(0, c)

    def end_job(c):
        if c < helped:

            @pl.when(helps)
            def _():
                end_out[c] = received(1, c).astype(jnp.bfloat16)
                end_copy(c, end_z).start()

        put(c, received(0, c))

    def degrees():
        for k in range(1, reps):
            r = lax.rem(me + k, reps)
            deg_copy(r, r).wait_recv()
        degree = deg_in[0]
        for r in range(1, reps):
            degree += deg_in[r]
        scale[...] = jnp.broadcast_to(degree[0:1, :] + 1.0, (CHUNK, own)).T

    for c in range(chunks):

        def step(c=c):
            gather(c)
            start_job(c)

        when(takes(c), step)
        if c == 0:
            degrees()
        if c > 0:
            when(takes(c - 1), lambda: end_job(c - 1))
    if helped:

        @pl.when(at_end)
        def _():
            for c in range(helped):
                end_copy(c, helper_z).wait_recv()
                put(c, end_in[c].astype(jnp.float32))

    end_job(chunks - 1)

    for k in range(1, reps):
        deg_copy(lax.rem(me + k, reps), me).wait_send()
    if helped:

        @pl.when(at_end)
        def _():
            for kind in range(3):
                list_copy(kind, helper_z).wait_send()

    def job_left(job):
        if cores == 2:
            sib_copy(job).wait_send()
        for k in range(1, chips):
            chip_copy(job, lax.rem(chip + k, chips), chip).wait_send()

    for c in range(chunks):
        when(takes(c), lambda: job_left(c))
        if c < helped:

            @pl.when(helps)
            def _():
                job_left(chunks + c)
                end_copy(c, end_z).wait_send()

        def drain(source):
            when(
                jnp.logical_and(sends(c, True), source <= z),
                lambda: shift(source, c, True).wait_send(),
            )
            when(
                jnp.logical_and(sends(c, False), source >= z),
                lambda: shift(source, c, False).wait_send(),
            )

        repeat(loops, drain)


def body(features, weight, block_row, edge_row, edge_col, edge_count):
    loops = lax.axis_size("loop")
    reps = lax.axis_size("rep")
    own, width = features.shape
    chunks = width // CHUNK
    slots, edges = edge_row.shape[3:]
    chips = reps // 2 if reps % 2 == 0 else reps
    helped = 0
    kinds = 2 if helped else 1
    jobs = chunks + helped
    listing = (slots, loops, edges)
    dma = pltpu.SemaphoreType.DMA
    bf16, f32, i32 = jnp.bfloat16, jnp.float32, jnp.int32

    def stored(array):
        return jnp.swapaxes(array.reshape(loops, slots, edges), 0, 1)

    normalized = pl.pallas_call(
        functools.partial(kernel, loops, reps, helped),
        out_shape=jax.ShapeDtypeStruct((own, width), bf16),
        in_specs=[pl.BlockSpec(memory_space=pl.ANY)] * 5,
        out_specs=pl.BlockSpec(memory_space=pltpu.VMEM),
        scratch_shapes=[
            pltpu.VMEM((chunks, loops * own, CHUNK), bf16),
            pltpu.VMEM((kinds, reps * own, loops * own), bf16),
            pltpu.VMEM((kinds, chips, own, CHUNK), f32),
            pltpu.VMEM((jobs, chips, own, CHUNK), bf16),
            pltpu.VMEM((jobs, chips, own, CHUNK), bf16),
            pltpu.VMEM((jobs, chips, own, CHUNK), bf16),
            pltpu.VMEM((jobs, chips, own, CHUNK), bf16),
            pltpu.VMEM((jobs, own, CHUNK), f32),
            pltpu.VMEM((max(helped, 1), own, CHUNK), bf16),
            pltpu.VMEM((max(helped, 1), own, CHUNK), bf16),
            pltpu.VMEM((reps, 8, own), f32),
            pltpu.VMEM((reps, 8, own), f32),
            pltpu.VMEM((own, CHUNK), f32),
            pltpu.VMEM((loops, slots), i32),
            pltpu.VMEM((3,) + listing, i32),
            pltpu.VMEM((3,) + listing, i32),
            dma((4 + chunks,)),
            dma((loops, chunks)),
            dma((loops, chunks)),
            dma((loops, chunks)),
            dma((jobs,)),
            dma((jobs,)),
            dma((jobs, chips)),
            dma((jobs, chips)),
            dma((max(helped, 1),)),
            dma((max(helped, 1),)),
            dma((3,)),
            dma((3,)),
            dma((reps,)),
            dma((reps,)),
        ],
        compiler_params=pltpu.CompilerParams(
            collective_id=0, has_side_effects=True, vmem_limit_bytes=56 * 1024 * 1024
        ),
    )(
        features,
        block_row.reshape(loops, slots),
        stored(edge_row),
        stored(edge_col),
        stored(edge_count),
    )
    product = jnp.dot(normalized, weight, preferred_element_type=f32)
    return jnp.maximum(product, 0.0).astype(bf16)


def solution(mesh):
    return jax.shard_map(
        body,
        mesh=mesh,
        in_specs=(
            P(("groups", "loop", "rep"), None),
            P(),
            P(("groups", "loop"), "rep", None, None),
            P(("groups", "loop"), "rep", None, None, None),
            P(("groups", "loop"), "rep", None, None, None),
            P(("groups", "loop"), "rep", None, None, None),
        ),
        out_specs=P(("groups", "loop", "rep"), None),
        check_vma=False,
    )
```
